32 devices in a mesh: dom: 2 (over x), row: 8 (over z, y), col: 2 (over core).
Axes of the slice: x: 2, y: 2, z: 4, core: 2. Of those that a mesh axis runs over, the one named last changes fastest.
Arguments:
- pair: bfloat16 [224, 112, 128], P(('dom', 'row'), 'col'), parts along dimension 0, may hold values from -6 to 6
- length: int32 [2], P('dom'), parts along dimension 0, may hold values from 56 to 112
- w_tri_in: bfloat16 [128, 640], replicated, may hold values from -0.5 to 0.5
- w_tri_out: bfloat16 [128, 128], replicated, may hold values from -0.5 to 0.5
- w_att: bfloat16 [128, 512], replicated, may hold values from -4 to 4
- w_bias: bfloat16 [128, 4], replicated, may hold values from -0.5 to 0.5
- w_att_out: bfloat16 [128, 128], replicated, may hold values from -0.5 to 0.5
- w_up: bfloat16 [128, 1024], replicated, may hold values from -0.5 to 0.5
- w_down: bfloat16 [512, 128], replicated, may hold values from -0.25 to 0.25
Outputs:
- pair_out: bfloat16 [224, 112, 128], P(('dom', 'row', 'col')), parts along dimension 0
The draws below stay inside these ranges and needn't reach their ends.
There are 2 independent parts, one for each index of `dom`. The reference program is written for one: setup_inputs(seed, part) draws one part's arguments, and reference() takes and returns one part's arrays. A program takes and returns all parts, laid end to end along the dimension named above; an argument that names none is the same for every part. Nothing has to cross between parts.
All inputs are finite; a program needn't handle non-finite values.
Results may differ from the reference program's by a relative error of at most 0.012.
Values may be sent and summed in bfloat16 or wider, within the bound.
A program may use at most 192 MiB of HBM per device.

```python
import jax
import jax.numpy as jnp
from jax import lax

C = 128
HEADS = 4
HEAD_DIM = 32
FFH = 512
N = 112


def draw_w_att(key, part):
    key = jax.random.fold_in(key, 11)
    weights_drawn = jax.random.normal(jax.random.fold_in(key, 1), (C, 4 * C), jnp.float32) * C ** (-0.5)
    return jnp.clip(weights_drawn, -4.0, 4.0).astype(jnp.bfloat16)


def steps_of(stream_key, dims, pieces, least, top_value):
    loudness, own = 1.0, jax.random.fold_in(stream_key, 6)
    for axis_at, parts in pieces:
        draws = jnp.exp(jax.random.uniform(jax.random.fold_in(own, axis_at), (parts,), jnp.float32, least / len(pieces), top_value / len(pieces)))
        loudness = loudness * jnp.repeat(draws, dims[axis_at] // parts).reshape([-1 if axis == axis_at else 1 for axis in range(len(dims))])
    return loudness


def scatter_about(rng, shape, deviation, bound, pieces=(), kind=jnp.bfloat16):
    factor_of = steps_of(rng, shape, pieces, -0.22, 0.18) if pieces else 1.0
    entries = jax.random.normal(rng, shape, jnp.float32) * deviation * factor_of
    return jnp.minimum(jnp.maximum(entries, -bound), bound).astype(kind)


def setup_inputs(seed: int = 0, part: int = 0) -> dict:
    keys = jax.random.split(jax.random.key(seed), 10)
    own_keys = jax.random.split(jax.random.fold_in(keys[9], part), 10)
    pair = scatter_about(own_keys[0], (N, N, C), 1.0, 6.0, ((0, 8), (1, 2)))
    length = jax.random.randint(own_keys[1], (1,), N // 2, N + 1).astype(jnp.int32)
    w_tri_in = scatter_about(keys[2], (C, 5 * C), C ** -0.5, 0.5)
    w_tri_out = scatter_about(keys[3], (C, C), C ** -0.5, 0.5)
    w_att = draw_w_att(jax.random.fold_in(keys[9], 71), part)
    w_bias = scatter_about(keys[5], (C, HEADS), C ** -0.5, 0.5)
    w_att_out = scatter_about(keys[6], (C, C), C ** -0.5, 0.5)
    w_up = scatter_about(keys[7], (C, 2 * FFH), C ** -0.5, 0.5)
    w_down = scatter_about(keys[8], (FFH, C), FFH ** -0.5, 0.25)
    return dict(pair=pair, length=length, w_tri_in=w_tri_in, w_tri_out=w_tri_out, w_att=w_att, w_bias=w_bias, w_att_out=w_att_out, w_up=w_up, w_down=w_down)


def layer_norm(values_in):
    average = lax.optimization_barrier(jnp.mean(values_in, axis=-1, keepdims=True))
    centered = values_in - average
    variance = lax.optimization_barrier(jnp.mean(centered * centered, axis=-1, keepdims=True))
    return centered * lax.rsqrt(variance + 1e-05)

def project(operand, weight):
    flat = operand.reshape(-1, operand.shape[-1])
    product = jnp.dot(flat, weight, preferred_element_type=jnp.float32)
    return product.reshape(operand.shape[:-1] + (weight.shape[1],))

def reference(pair, length, w_tri_in, w_tri_out, w_att, w_bias, w_att_out, w_up, w_down):
    token_count = pair.shape[0]
    valid_length = length[0]
    token_keep = jnp.arange(token_count, dtype=jnp.int32) < valid_length
    cell_keep = (token_keep[:, None] & token_keep[None, :]).astype(jnp.float32)[:, :, None]
    residual = pair.astype(jnp.float32)
    normed = layer_norm(residual).astype(jnp.bfloat16)
    projected = project(normed, w_tri_in).reshape(token_count, token_count, 5, C)
    left_edge = (cell_keep * jax.nn.sigmoid(projected[:, :, 1]) * projected[:, :, 0]).astype(jnp.bfloat16)
    right_edge = (cell_keep * jax.nn.sigmoid(projected[:, :, 3]) * projected[:, :, 2]).astype(jnp.bfloat16)
    out_gate = jax.nn.sigmoid(projected[:, :, 4])
    tri_sum = jnp.einsum('ikc,jkc->ijc', left_edge.astype(jnp.float32), right_edge.astype(jnp.float32))
    tri_norm = layer_norm(tri_sum).astype(jnp.bfloat16)
    after_tri = (residual + out_gate * project(tri_norm, w_tri_out)).astype(jnp.bfloat16)
    tri_f = after_tri.astype(jnp.float32)
    slab_norm = layer_norm(tri_f).astype(jnp.bfloat16)
    att_proj = project(slab_norm, w_att).reshape(token_count, token_count, 4, C)
    queries = (att_proj[:, :, 0] * HEAD_DIM ** (-0.5)).astype(jnp.bfloat16).reshape(token_count, token_count, HEADS, HEAD_DIM)
    key_rows = att_proj[:, :, 1].astype(jnp.bfloat16).reshape(token_count, token_count, HEADS, HEAD_DIM)
    values = att_proj[:, :, 2].astype(jnp.bfloat16).reshape(token_count, token_count, HEADS, HEAD_DIM)
    att_gate = jax.nn.sigmoid(att_proj[:, :, 3])
    pair_bias = jnp.transpose(project(slab_norm, w_bias), (2, 0, 1)).astype(jnp.bfloat16).astype(jnp.float32)

    def one_row(row_items):
        query_row, key_row, value_row = row_items
        scores = jnp.einsum('jhd,khd->hjk', query_row.astype(jnp.float32), key_row.astype(jnp.float32)) + pair_bias
        scores = jnp.where(token_keep[None, None, :], scores, jnp.float32(-1000000000.0))
        peak = lax.optimization_barrier(jnp.max(scores, axis=-1, keepdims=True))
        expo = jnp.exp(scores - peak)
        weights = (expo / lax.optimization_barrier(jnp.sum(expo, axis=-1, keepdims=True))).astype(jnp.bfloat16)
        mixed = jnp.einsum('hjk,khd->jhd', weights.astype(jnp.float32), value_row.astype(jnp.float32))
        return mixed.reshape(token_count, C)
    attended = lax.map(one_row, (queries, key_rows, values))
    gated_out = (att_gate * attended).astype(jnp.bfloat16)
    second = (tri_f + project(gated_out, w_att_out)).astype(jnp.bfloat16)
    second_f = second.astype(jnp.float32)
    hidden = project(layer_norm(second_f).astype(jnp.bfloat16), w_up)
    activated = (jax.nn.silu(hidden[..., :FFH]) * hidden[..., FFH:]).astype(jnp.bfloat16)
    return (second_f + project(activated, w_down)).astype(jnp.bfloat16)
```

```python
import functools

import jax
import jax.numpy as jnp
from jax import lax
from jax.experimental import pallas as pl
from jax.experimental.pallas import tpu as pltpu
from jax.sharding import PartitionSpec as P

HEADS = 4
F32 = jnp.float32
BF16 = jnp.bfloat16
MESH = pl.DeviceIdType.MESH


def layer_norm(values_in):
    average = jnp.mean(values_in, axis=-1, keepdims=True)
    centered = values_in - average
    variance = jnp.mean(centered * centered, axis=-1, keepdims=True)
    return centered * lax.rsqrt(variance + 1e-05)


def mul(left, right):
    return jnp.dot(left, right, preferred_element_type=F32)


def mul_t(left, right):
    return lax.dot_general(left, right, (((1,), (1,)), ((), ())), preferred_element_type=F32)


def kernel(
    rows_n,
    length_ref,
    pair_ref,
    w_tri_in,
    w_tri_out,
    w_att,
    w_bias,
    w_att_out,
    w_up,
    w_down,
    out_ref,
    normed,
    right_all,
    left_f,
    pair_other,
    gate,
    acc,
    part_out,
    part_in,
    after,
    slab,
    keys_s,
    values_s,
    queries_s,
    att_gate,
    bias_own,
    bias_all,
    bias_f,
    ring_send,
    ring_recv,
    part_send,
    part_recv,
    pair_send,
    pair_recv,
    bias_send,
    bias_recv,
):
    rows, cols, channels = pair_ref.shape
    full = 2 * cols
    padded = slab.shape[1]
    slab_rows = rows // 2
    hidden_units = w_down.shape[0]
    head_size = channels // HEADS
    peers = 2 * rows_n
    half_ring = rows_n // 2
    pair_cells = 2 * cols
    cells = rows * cols
    first_pairs = (rows + 2) // 4
    parts = ((0, first_pairs), (first_pairs, rows // 2 - first_pairs))
    snake = rows_n <= 8

    row = lax.axis_index("row")
    col = lax.axis_index("col")
    me = row * 2 + col

    def place(r):
        if not snake:
            return r
        return jnp.where(r % 2 == 0, r // 2, rows_n - 1 - r // 2)

    def owner_at(p):
        p = lax.rem(p + 2 * rows_n, rows_n)
        if not snake:
            return p
        return jnp.where(p < rows_n // 2, 2 * p, 2 * (rows_n - p) - 1)

    pos = place(row)
    nexts = (owner_at(pos + 1), owner_at(pos - 1))

    barrier = pltpu.get_barrier_semaphore()

    def greet(t, carry):
        peer = lax.rem(me + t, peers)
        pl.semaphore_signal(
            barrier, inc=1, device_id={"row": peer // 2, "col": peer % 2}, device_id_type=MESH
        )
        return carry

    lax.fori_loop(1, peers, greet, 0)

    length = length_ref[0]
    row_off = row * rows
    col_off = col * cols
    flat = lax.broadcasted_iota(jnp.int32, (pair_cells, channels), 0)
    second_row = (flat >= cols).astype(jnp.int32)
    col_ok = col_off + flat - cols * second_row < length

    def keep_of(p):
        return col_ok & (row_off + 2 * p + second_row < length)

    def right_step(p, carry):
        block = pair_ref[pl.ds(2 * p, 2)].astype(F32).reshape(pair_cells, channels)
        norm = layer_norm(block).astype(BF16)
        at = pl.ds(pl.multiple_of(p * pair_cells, 16), pair_cells)
        normed[at, :] = norm
        proj = mul(norm, w_tri_in[:, 2 * channels : 4 * channels])
        edge = jax.nn.sigmoid(proj[:, channels:]) * proj[:, :channels]
        to = pl.ds(pl.multiple_of(row * cells + p * pair_cells, 16), pair_cells)
        right_all[to, :] = jnp.where(keep_of(p), edge, 0.0).astype(BF16)
        return carry

    def ring_copy(way, dist, part, owner):
        start, count = parts[part]
        at = pl.ds(
            pl.multiple_of(owner * cells + start * pair_cells, 16), count * pair_cells
        )
        return pltpu.make_async_remote_copy(
            src_ref=right_all.at[at],
            dst_ref=right_all.at[at],
            send_sem=ring_send.at[way, dist, part],
            recv_sem=ring_recv.at[way, dist, part],
            device_id={"row": nexts[way]},
            device_id_type=MESH,
        )

    pair_copy = pltpu.make_async_remote_copy(
        src_ref=pair_ref.at[pl.ds((1 - col) * slab_rows, slab_rows)],
        dst_ref=pair_other,
        send_sem=pair_send,
        recv_sem=pair_recv,
        device_id={"col": 1 - col},
        device_id_type=MESH,
    )

    lax.fori_loop(0, first_pairs, right_step, 0)
    pl.semaphore_wait(barrier, peers - 1)
    ring_copy(0, 1, 0, row).start()
    ring_copy(1, 1, 0, row).start()
    pair_copy.start()
    lax.fori_loop(first_pairs, rows // 2, right_step, 0)
    ring_copy(0, 1, 1, row).start()
    ring_copy(1, 1, 1, row).start()

    def left_step(p, carry):
        at = pl.ds(pl.multiple_of(p * pair_cells, 16), pair_cells)
        proj = mul(normed[at, :], w_tri_in[:, : 2 * channels])
        edge = jax.nn.sigmoid(proj[:, channels:]) * proj[:, :channels]
        edge = jnp.where(keep_of(p), edge, 0.0).astype(BF16).astype(F32)
        left_f[pl.ds(2 * p, 2)] = edge.reshape(2, cols, channels)
        return carry

    lax.fori_loop(0, rows // 2, left_step, 0)

    def part_copy(part, owner):
        start, count = parts[part]
        at = pl.ds(pl.multiple_of((owner * rows + 2 * start) * 8, 16), 16 * count)
        return pltpu.make_async_remote_copy(
            src_ref=part_out.at[at],
            dst_ref=part_in.at[at],
            send_sem=part_send.at[owner, part],
            recv_sem=part_recv.at[owner, part],
            device_id={"col": 1 - col},
            device_id_type=MESH,
        )

    def tri_part(part, owner):
        start, count = parts[part]

        def step(p, carry):
            at = pl.ds(pl.multiple_of(owner * cells + p * pair_cells, 16), pair_cells)
            both = right_all[at, :].astype(F32).reshape(2, cols, channels)
            for side, ref in ((1 - col, part_out), (col, acc)):
                block = left_f[pl.ds(side * slab_rows, slab_rows)]
                for t in range(2):
                    total = jnp.sum(block * both[t][None], axis=1)
                    to = pl.multiple_of((owner * rows + 2 * p + t) * 8, 8)
                    ref[pl.ds(to, slab_rows), :] = total
            return carry

        lax.fori_loop(start, start + count, step, 0)
        part_copy(part, owner).start()

    tri_part(0, row)
    tri_part(1, row)

    pair_copy.wait_recv()

    def whole_row(i):
        own = pair_ref[col * slab_rows + i].astype(F32)
        other = pair_other[i].astype(F32)
        low = jnp.where(col == 0, own, other)
        high = jnp.where(col == 0, other, own)
        return jnp.concatenate([low, high], axis=0)

    def gate_step(i, carry):
        whole = whole_row(i)
        after[i] = whole
        norm = layer_norm(whole).astype(BF16)
        gate[i] = jax.nn.sigmoid(mul(norm, w_tri_in[:, 4 * channels :]))
        return carry

    lax.fori_loop(0, slab_rows, gate_step, 0)

    def ring_step(s, carry):
        owners = (owner_at(pos - s), owner_at(pos + s))
        for part in range(2):
            for way in range(2):
                ring_copy(way, s, part, owners[way]).wait_recv()
                if part == way:
                    ring_copy(way, s + 1, part, owners[way]).start()
                else:

                    @pl.when(s < half_ring - 1)
                    def _():
                        ring_copy(way, s + 1, part, owners[way]).start()

            tri_part(part, owners[0])
            tri_part(part, owners[1])
        return carry

    lax.fori_loop(1, half_ring, ring_step, 0)
    far = owner_at(pos + half_ring)
    for part in range(2):
        ring_copy(part, half_ring, part, far).wait_recv()
        tri_part(part, far)

    def part_wait(owner, carry):
        for part in range(2):
            part_copy(part, owner).wait_recv()
        return carry

    lax.fori_loop(0, rows_n, part_wait, 0)

    bias_own[...] = jnp.zeros_like(bias_own)

    def norm_step(i, carry):
        at = pl.ds(i, full, stride=8)
        summed = acc[at, :] + part_in[at, :]
        tri_norm = layer_norm(summed).astype(BF16)
        fresh = after[i] + gate[i] * mul(tri_norm, w_tri_out[...])
        fresh = fresh.astype(BF16).astype(F32)
        after[i] = fresh
        norm = layer_norm(fresh)
        if padded > full:
            norm = jnp.concatenate([norm, jnp.zeros((padded - full, channels), F32)], axis=0)
        norm = norm.astype(BF16)
        slab[i] = norm
        bias = mul_t(w_bias[...], norm)
        for h in range(HEADS):
            bias_own[pl.ds(8 * h + i, 1), :] = bias[h : h + 1]
        return carry

    lax.fori_loop(0, slab_rows, norm_step, 0)
    bias_all[me] = bias_own[...].astype(BF16)

    def bias_copy(t):
        peer = lax.rem(me + t, peers)
        return pltpu.make_async_remote_copy(
            src_ref=bias_all.at[me],
            dst_ref=bias_all.at[me],
            send_sem=bias_send.at[t],
            recv_sem=bias_recv.at[t],
            device_id={"row": peer // 2, "col": peer % 2},
            device_id_type=MESH,
        )

    def bias_arrival(t):
        peer = lax.rem(me + peers - t, peers)
        return pltpu.make_async_remote_copy(
            src_ref=bias_all.at[peer],
            dst_ref=bias_all.at[peer],
            send_sem=bias_send.at[t],
            recv_sem=bias_recv.at[t],
            device_id={"row": peer // 2, "col": peer % 2},
            device_id_type=MESH,
        )

    def bias_start(t, carry):
        bias_copy(t).start()
        return carry

    lax.fori_loop(1, peers, bias_start, 0)

    head_of = lax.broadcasted_iota(jnp.int32, (full, channels), 1) // head_size

    def att_step(i, carry):
        proj = mul(slab[i], w_att[...])
        queries_s[i] = (proj[:full, :channels] * head_size ** (-0.5)).astype(BF16)
        keys_s[i] = proj[:, channels : 2 * channels].astype(BF16)
        values_s[i, :, :channels] = proj[:, 2 * channels : 3 * channels].astype(BF16)
        values_s[i, :, channels:] = jnp.ones((padded, channels), BF16)
        att_gate[i] = jax.nn.sigmoid(proj[:full, 3 * channels :])
        return carry

    lax.fori_loop(0, slab_rows, att_step, 0)

    def bias_wait(t, carry):
        bias_arrival(t).wait_recv()
        return carry

    lax.fori_loop(1, peers, bias_wait, 0)
    key_ok = lax.broadcasted_iota(jnp.int32, (slab_rows, padded), 1) < length
    for peer in range(peers):
        block = bias_all[peer].astype(F32)
        for h in range(HEADS):
            bias_f[h, peer * slab_rows : (peer + 1) * slab_rows, :] = jnp.where(
                key_ok, block[8 * h : 8 * h + slab_rows], -1000000000.0
            )

    def row_step(i, carry):
        query = queries_s[i].astype(F32)
        key = keys_s[i]
        value = values_s[i]
        top = jnp.zeros((full, channels), F32)
        bottom = jnp.zeros((full, channels), F32)
        for h in range(HEADS):
            mine = head_of == h
            scores = mul_t(jnp.where(mine, query, 0.0).astype(BF16), key) + bias_f[h]
            peak = jnp.max(scores, axis=-1, keepdims=True)
            expo = jnp.exp(scores - peak).astype(BF16)
            mixed = mul(expo, value)
            top = jnp.where(mine, mixed[:, :channels], top)
            bottom = jnp.where(mine, mixed[:, channels:], bottom)
        gated = (att_gate[i] * (top / bottom)).astype(BF16)
        second = (after[i] + mul(gated, w_att_out[...])).astype(BF16).astype(F32)
        hidden = mul(layer_norm(second).astype(BF16), w_up[...])
        activated = jax.nn.silu(hidden[:, :hidden_units]) * hidden[:, hidden_units:]
        result = second + mul(activated.astype(BF16), w_down[...])
        out_ref[i] = result.astype(BF16)
        return carry

    lax.fori_loop(0, slab_rows, row_step, 0)

    pair_copy.wait_send()

    def ring_drain(s, carry):
        owners = (owner_at(pos - s), owner_at(pos + s))
        for way in range(2):
            for part in range(2):
                ring_copy(way, s + 1, part, owners[way]).wait_send()
        return carry

    lax.fori_loop(0, half_ring - 1, ring_drain, 0)
    ring_copy(0, half_ring, 0, owner_at(pos - half_ring + 1)).wait_send()
    ring_copy(1, half_ring, 1, owner_at(pos + half_ring - 1)).wait_send()

    def part_drain(owner, carry):
        for part in range(2):
            part_copy(part, owner).wait_send()
        return carry

    lax.fori_loop(0, rows_n, part_drain, 0)

    def bias_drain(t, carry):
        bias_copy(t).wait_send()
        return carry

    lax.fori_loop(1, peers, bias_drain, 0)


def shards(rows_n, pair, length, w_tri_in, w_tri_out, w_att, w_bias, w_att_out, w_up, w_down):
    rows, cols, channels = pair.shape
    full = 2 * cols
    padded = -(-full // 128) * 128
    slab_rows = rows // 2
    peers = 2 * rows_n
    half_ring = rows_n // 2
    bias_t = jnp.pad(w_bias.T, ((0, 16 - HEADS), (0, 0)))
    vmem = pl.BlockSpec(memory_space=pltpu.VMEM)
    dma = pltpu.SemaphoreType.DMA
    return pl.pallas_call(
        functools.partial(kernel, rows_n),
        out_shape=jax.ShapeDtypeStruct((slab_rows, full, channels), BF16),
        in_specs=[pl.BlockSpec(memory_space=pltpu.SMEM)] + [vmem] * 8,
        out_specs=vmem,
        scratch_shapes=[
            pltpu.VMEM((rows * cols, channels), BF16),
            pltpu.VMEM((rows_n * rows * cols, channels), BF16),
            pltpu.VMEM((rows, cols, channels), F32),
            pltpu.VMEM((slab_rows, cols, channels), BF16),
            pltpu.VMEM((slab_rows, full, channels), F32),
            pltpu.VMEM((full * 8, channels), F32),
            pltpu.VMEM((full * 8, channels), F32),
            pltpu.VMEM((full * 8, channels), F32),
            pltpu.VMEM((slab_rows, full, channels), F32),
            pltpu.VMEM((slab_rows, padded, channels), BF16),
            pltpu.VMEM((slab_rows, padded, channels), BF16),
            pltpu.VMEM((slab_rows, padded, 2 * channels), BF16),
            pltpu.VMEM((slab_rows, full, channels), BF16),
            pltpu.VMEM((slab_rows, full, channels), F32),
            pltpu.VMEM((HEADS * 8, padded), F32),
            pltpu.VMEM((peers, HEADS * 8, padded), BF16),
            pltpu.VMEM((HEADS, full, padded), F32),
            dma((2, half_ring + 1, 2)),
            dma((2, half_ring + 1, 2)),
            dma((rows_n, 2)),
            dma((rows_n, 2)),
            dma,
            dma,
            dma((peers,)),
            dma((peers,)),
        ],
        compiler_params=pltpu.CompilerParams(
            collective_id=0, has_side_effects=True, vmem_limit_bytes=60 * 2**20
        ),
    )(length, pair, w_tri_in, w_tri_out, w_att, bias_t, w_att_out, w_up, w_down)


def solution(mesh):
    placed = (P(("dom", "row"), "col", None), P("dom"), P(), P(), P(), P(), P(), P(), P())
    return jax.shard_map(
        functools.partial(shards, mesh.shape["row"]),
        mesh=mesh,
        in_specs=placed,
        out_specs=P(("dom", "row", "col"), None, None),
        check_vma=False,
    )
```

```python
import functools

import jax
import jax.numpy as jnp
from jax import lax
from jax.experimental import pallas as pl
from jax.experimental.pallas import tpu as pltpu
from jax.sharding import PartitionSpec as P

HEADS = 4
F32 = jnp.float32
BF16 = jnp.bfloat16
MESH = pl.DeviceIdType.MESH


def layer_norm(values_in):
    average = jnp.mean(values_in, axis=-1, keepdims=True)
    centered = values_in - average
    variance = jnp.mean(centered * centered, axis=-1, keepdims=True)
    return centered * lax.rsqrt(variance + 1e-05)


def mul(left, right):
    return jnp.dot(left, right, preferred_element_type=F32)


def mul_t(left, right):
    return lax.dot_general(left, right, (((1,), (1,)), ((), ())), preferred_element_type=F32)


def kernel(
    rows_n,
    length_ref,
    pair_ref,
    w_tri_in,
    w_tri_out,
    w_att,
    w_bias,
    w_att_out,
    w_up,
    w_down,
    out_ref,
    normed,
    right_all,
    left_f,
    pair_other,
    gate,
    acc,
    part_out,
    part_in,
    cells_f,
    scores_s,
    slab,
    keys_s,
    values_s,
    queries_s,
    att_gate,
    bias_own,
    bias_all,
    bias_f,
    ring_send,
    ring_recv,
    part_send,
    part_recv,
    pair_send,
    pair_recv,
    bias_send,
    bias_recv,
):
    rows, cols, channels = pair_ref.shape
    full = 2 * cols
    padded = slab.shape[1]
    slab_rows = rows // 2
    hidden_units = w_down.shape[0]
    head_size = channels // HEADS
    peers = 2 * rows_n
    half_ring = rows_n // 2
    pair_cells = 2 * cols
    cells = rows * cols
    pairs = rows // 2
    cuts = [0, (pairs + 2) // 4, (pairs + 1) // 2, (3 * pairs + 3) // 4, pairs]
    parts = tuple((a, b - a) for a, b in zip(cuts[:-1], cuts[1:]))
    orders = ((0, 1, 2, 3), (2, 3, 0, 1))
    early = scores_s.shape[1] == full
    snake = rows_n <= 8

    def loop(count, step):
        lax.fori_loop(0, count, step, 0, unroll=early)


    row = lax.axis_index("row")
    col = lax.axis_index("col")
    me = row * 2 + col

    def place(r):
        if not snake:
            return r
        return jnp.where(r % 2 == 0, r // 2, rows_n - 1 - r // 2)

    def owner_at(p):
        p = lax.rem(p + 2 * rows_n, rows_n)
        if not snake:
            return p
        return jnp.where(p < rows_n // 2, 2 * p, 2 * (rows_n - p) - 1)

    pos = place(row)
    nexts = (owner_at(pos + 1), owner_at(pos - 1))

    barrier = pltpu.get_barrier_semaphore()
    for way in range(2):
        pl.semaphore_signal(
            barrier, inc=1, device_id={"row": nexts[way]}, device_id_type=MESH
        )
    pl.semaphore_signal(barrier, inc=1, device_id={"col": 1 - col}, device_id_type=MESH)

    length = length_ref[0]
    row_off = row * rows
    col_off = col * cols
    flat = lax.broadcasted_iota(jnp.int32, (pair_cells, channels), 0)
    second_row = (flat >= cols).astype(jnp.int32)
    col_ok = col_off + flat - cols * second_row < length

    def keep_of(p):
        return col_ok & (row_off + 2 * p + second_row < length)

    def right_step(p, carry):
        block = pair_ref[pl.ds(2 * p, 2)].astype(F32).reshape(pair_cells, channels)
        norm = layer_norm(block).astype(BF16)
        at = pl.ds(pl.multiple_of(p * pair_cells, 16), pair_cells)
        normed[at, :] = norm
        proj = mul(norm, w_tri_in[:, 2 * channels : 4 * channels])
        edge = jax.nn.sigmoid(proj[:, channels:]) * proj[:, :channels]
        to = pl.ds(pl.multiple_of(row * cells + p * pair_cells, 16), pair_cells)
        right_all[to, :] = jnp.where(keep_of(p), edge, 0.0).astype(BF16)
        return carry

    def ring_copy(way, dist, part, owner):
        start, count = parts[part]
        at = pl.ds(
            pl.multiple_of(owner * cells + start * pair_cells, 16), count * pair_cells
        )
        return pltpu.make_async_remote_copy(
            src_ref=right_all.at[at],
            dst_ref=right_all.at[at],
            send_sem=ring_send.at[way, dist, part],
            recv_sem=ring_recv.at[way, dist, part],
            device_id={"row": nexts[way]},
            device_id_type=MESH,
        )

    pair_copy = pltpu.make_async_remote_copy(
        src_ref=pair_ref.at[pl.ds((1 - col) * slab_rows, slab_rows)],
        dst_ref=pair_other,
        send_sem=pair_send,
        recv_sem=pair_recv,
        device_id={"col": 1 - col},
        device_id_type=MESH,
    )

    lax.fori_loop(0, pairs, right_step, 0)
    pl.semaphore_wait(barrier, 3)
    for turn in range(4):
        for way in range(2):
            ring_copy(way, 1, orders[way][turn], row).start()
    pair_copy.start()

    def left_step(p, carry):
        at = pl.ds(pl.multiple_of(p * pair_cells, 16), pair_cells)
        proj = mul(normed[at, :], w_tri_in[:, : 2 * channels])
        edge = jax.nn.sigmoid(proj[:, channels:]) * proj[:, :channels]
        edge = jnp.where(keep_of(p), edge, 0.0).astype(BF16).astype(F32)
        left_f[pl.ds(2 * p, 2)] = edge.reshape(2, cols, channels)
        return carry

    lax.fori_loop(0, rows // 2, left_step, 0)

    def part_copy(part, owner):
        start, count = parts[part]
        at = pl.ds(pl.multiple_of((owner * rows + 2 * start) * 8, 16), 16 * count)
        return pltpu.make_async_remote_copy(
            src_ref=part_out.at[at],
            dst_ref=part_in.at[at],
            send_sem=part_send.at[owner, part],
            recv_sem=part_recv.at[owner, part],
            device_id={"col": 1 - col},
            device_id_type=MESH,
        )

    def tri_part(part, owner):
        start, count = parts[part]

        def step(p, carry):
            at = pl.ds(pl.multiple_of(owner * cells + p * pair_cells, 16), pair_cells)
            both = right_all[at, :].astype(F32).reshape(2, cols, channels)
            for side, ref in ((1 - col, part_out), (col, acc)):
                block = left_f[pl.ds(side * slab_rows, slab_rows)]
                for t in range(2):
                    total = jnp.sum(block * both[t][None], axis=1)
                    to = pl.multiple_of((owner * rows + 2 * p + t) * 8, 8)
                    ref[pl.ds(to, slab_rows), :] = total
            return carry

        lax.fori_loop(start, start + count, step, 0)
        part_copy(part, owner).start()

    for part in range(4):
        tri_part(part, row)

    pair_copy.wait_recv()

    def whole_row(i):
        own = pair_ref[col * slab_rows + i].astype(F32)
        other = pair_other[i].astype(F32)
        low = jnp.where(col == 0, own, other)
        high = jnp.where(col == 0, other, own)
        return jnp.concatenate([low, high], axis=0)

    def gate_step(i, carry):
        whole = whole_row(i)
        at = pl.ds(i, full, stride=8)
        cells_f[at, :] = whole
        norm = layer_norm(whole).astype(BF16)
        gate[at, :] = jax.nn.sigmoid(mul(norm, w_tri_in[:, 4 * channels :]))
        return carry

    lax.fori_loop(0, slab_rows, gate_step, 0)

    def finish(owner):
        for part in range(4):
            part_copy(part, owner).wait_recv()
        at = pl.ds(pl.multiple_of(owner * rows * 8, 16), rows * 8)
        tri_norm = layer_norm(acc[at, :] + part_in[at, :]).astype(BF16)
        fresh = cells_f[at, :] + gate[at, :] * mul(tri_norm, w_tri_out[...])
        fresh = fresh.astype(BF16).astype(F32)
        acc[at, :] = fresh
        cells_f[at, :] = layer_norm(fresh)

    def ring_step(s, carry):
        owners = (owner_at(pos - s), owner_at(pos + s))
        for turn in range(4):
            for way in range(2):
                part = orders[way][turn]
                ring_copy(way, s, part, owners[way]).wait_recv()
                if turn < 2:
                    ring_copy(way, s + 1, part, owners[way]).start()
                else:

                    @pl.when(s < half_ring - 1)
                    def _():
                        ring_copy(way, s + 1, part, owners[way]).start()

            for way in range(2):
                tri_part(orders[way][turn], owners[way])
        finish(owner_at(pos - s + 1))

        @pl.when(s > 1)
        def _():
            finish(owner_at(pos + s - 1))

        return carry

    lax.fori_loop(1, half_ring, ring_step, 0)
    finish(owner_at(pos - half_ring + 1))
    finish(owner_at(pos + half_ring - 1))
    far = owner_at(pos + half_ring)
    for turn in range(2):
        for way in range(2):
            ring_copy(way, half_ring, orders[way][turn], far).wait_recv()
            tri_part(orders[way][turn], far)
    finish(far)

    bias_own[...] = jnp.zeros_like(bias_own)
    bias_w = jnp.concatenate(
        [w_bias[...].astype(F32).T, jnp.zeros((16 - HEADS, channels), F32)], axis=0
    ).astype(BF16)

    def norm_step(i, carry):
        norm = cells_f[pl.ds(i, full, stride=8), :]
        if padded > full:
            norm = jnp.concatenate([norm, jnp.zeros((padded - full, channels), F32)], axis=0)
        norm = norm.astype(BF16)
        slab[i] = norm
        bias = mul_t(bias_w, norm)
        for h in range(HEADS):
            bias_own[pl.ds(8 * h + i, 1), :] = bias[h : h + 1]
        return carry

    loop(slab_rows, norm_step)
    bias_all[me] = bias_own[...].astype(BF16)

    def bias_copy(t):
        peer = lax.rem(me + t, peers)
        return pltpu.make_async_remote_copy(
            src_ref=bias_all.at[me],
            dst_ref=bias_all.at[me],
            send_sem=bias_send.at[t],
            recv_sem=bias_recv.at[t],
            device_id={"row": peer // 2, "col": peer % 2},
            device_id_type=MESH,
        )

    def bias_arrival(t):
        peer = lax.rem(me + peers - t, peers)
        return pltpu.make_async_remote_copy(
            src_ref=bias_all.at[peer],
            dst_ref=bias_all.at[peer],
            send_sem=bias_send.at[t],
            recv_sem=bias_recv.at[t],
            device_id={"row": peer // 2, "col": peer % 2},
            device_id_type=MESH,
        )

    def bias_start(t, carry):
        bias_copy(t).start()
        return carry

    lax.fori_loop(1, peers, bias_start, 0)

    head_of = lax.broadcasted_iota(jnp.int32, (full, channels), 1) // head_size

    def score(h, query, key):
        query = jnp.where(head_of == h, query.astype(F32), 0.0).astype(BF16)
        return mul_t(query, key)

    def att_step(i, carry):
        proj = mul(slab[i], w_att[...])
        query = (proj[:full, :channels] * head_size ** (-0.5)).astype(BF16)
        key = proj[:, channels : 2 * channels].astype(BF16)
        if early:
            for h in range(HEADS):
                scores_s[i * HEADS + h] = score(h, query, key)
        else:
            queries_s[i] = query
            keys_s[i] = key
        values_s[i, :, :channels] = proj[:, 2 * channels : 3 * channels].astype(BF16)
        values_s[i, :, channels:] = jnp.ones((padded, channels), BF16)
        att_gate[i] = jax.nn.sigmoid(proj[:full, 3 * channels :])
        return carry

    loop(slab_rows, att_step)

    def bias_wait(t, carry):
        bias_arrival(t).wait_recv()
        return carry

    lax.fori_loop(1, peers, bias_wait, 0)
    key_ok = lax.broadcasted_iota(jnp.int32, (slab_rows, padded), 1) < length
    for peer in range(peers):
        block = bias_all[peer].astype(F32)
        for h in range(HEADS):
            bias_f[h, peer * slab_rows : (peer + 1) * slab_rows, :] = jnp.where(
                key_ok, block[8 * h : 8 * h + slab_rows], -1000000000.0
            )

    def row_step(i, carry):
        value = values_s[i]
        top = jnp.zeros((full, channels), F32)
        bottom = jnp.zeros((full, channels), F32)
        for h in range(HEADS):
            mine = head_of == h
            if early:
                scores = scores_s[i * HEADS + h] + bias_f[h]
            else:
                scores = score(h, queries_s[i], keys_s[i]) + bias_f[h]
            peak = jnp.max(scores, axis=-1, keepdims=True)
            expo = jnp.exp(scores - peak).astype(BF16)
            mixed = mul(expo, value)
            top = jnp.where(mine, mixed[:, :channels], top)
            bottom = jnp.where(mine, mixed[:, channels:], bottom)
        gated = (att_gate[i] * (top / bottom)).astype(BF16)
        second = (acc[pl.ds(i, full, stride=8), :] + mul(gated, w_att_out[...])).astype(BF16).astype(F32)
        hidden = mul(layer_norm(second).astype(BF16), w_up[...])
        activated = jax.nn.silu(hidden[:, :hidden_units]) * hidden[:, hidden_units:]
        result = second + mul(activated.astype(BF16), w_down[...])
        out_ref[i] = result
        return carry

    loop(slab_rows, row_step)

    pair_copy.wait_send()

    def ring_drain(s, carry):
        owners = (owner_at(pos - s), owner_at(pos + s))
        for way in range(2):
            for part in range(4):
                ring_copy(way, s + 1, part, owners[way]).wait_send()
        return carry

    lax.fori_loop(0, half_ring - 1, ring_drain, 0)
    lasts = (owner_at(pos - half_ring + 1), owner_at(pos + half_ring - 1))
    for way in range(2):
        for turn in range(2):
            ring_copy(way, half_ring, orders[way][turn], lasts[way]).wait_send()

    def part_drain(owner, carry):
        for part in range(4):
            part_copy(part, owner).wait_send()
        return carry

    lax.fori_loop(0, rows_n, part_drain, 0)

    def bias_drain(t, carry):
        bias_copy(t).wait_send()
        return carry

    lax.fori_loop(1, peers, bias_drain, 0)


def shards(rows_n, pair, length, w_tri_in, w_tri_out, w_att, w_bias, w_att_out, w_up, w_down):
    rows, cols, channels = pair.shape
    full = 2 * cols
    padded = -(-full // 128) * 128
    slab_rows = rows // 2
    peers = 2 * rows_n
    half_ring = rows_n // 2
    kept = (slab_rows * HEADS, full, padded) if full <= 128 else (1, 8, 128)
    vmem = pl.BlockSpec(memory_space=pltpu.VMEM)
    dma = pltpu.SemaphoreType.DMA
    result = pl.pallas_call(
        functools.partial(kernel, rows_n),
        out_shape=jax.ShapeDtypeStruct((slab_rows, full, channels), F32),
        in_specs=[pl.BlockSpec(memory_space=pltpu.SMEM)] + [vmem] * 8,
        out_specs=vmem,
        scratch_shapes=[
            pltpu.VMEM((rows * cols, channels), BF16),
            pltpu.VMEM((rows_n * rows * cols, channels), BF16),
            pltpu.VMEM((rows, cols, channels), F32),
            pltpu.VMEM((slab_rows, cols, channels), BF16),
            pltpu.VMEM((full * 8, channels), F32),
            pltpu.VMEM((full * 8, channels), F32),
            pltpu.VMEM((full * 8, channels), F32),
            pltpu.VMEM((full * 8, channels), F32),
            pltpu.VMEM((full * 8, channels), F32),
            pltpu.VMEM(kept, F32),
            pltpu.VMEM((slab_rows, padded, channels), BF16),
            pltpu.VMEM((slab_rows, padded, channels), BF16),
            pltpu.VMEM((slab_rows, padded, 2 * channels), BF16),
            pltpu.VMEM((slab_rows, full, channels), BF16),
            pltpu.VMEM((slab_rows, full, channels), F32),
            pltpu.VMEM((HEADS * 8, padded), F32),
            pltpu.VMEM((peers, HEADS * 8, padded), BF16),
            pltpu.VMEM((HEADS, full, padded), F32),
            dma((2, half_ring + 1, 4)),
            dma((2, half_ring + 1, 4)),
            dma((rows_n, 4)),
            dma((rows_n, 4)),
            dma,
            dma,
            dma((peers,)),
            dma((peers,)),
        ],
        compiler_params=pltpu.CompilerParams(
            collective_id=0, has_side_effects=True, vmem_limit_bytes=60 * 2**20
        ),
    )(length, pair, w_tri_in, w_tri_out, w_att, w_bias, w_att_out, w_up, w_down)
    return result.astype(BF16)


def solution(mesh):
    placed = (P(("dom", "row"), "col", None), P("dom"), P(), P(), P(), P(), P(), P(), P())
    return jax.shard_map(
        functools.partial(shards, mesh.shape["row"]),
        mesh=mesh,
        in_specs=placed,
        out_specs=P(("dom", "row", "col"), None, None),
        check_vma=False,
    )
```

```python
import functools

import jax
import jax.numpy as jnp
from jax import lax
from jax.experimental import pallas as pl
from jax.experimental.pallas import tpu as pltpu
from jax.sharding import PartitionSpec as P

HEADS = 4
F32 = jnp.float32
BF16 = jnp.bfloat16
MESH = pl.DeviceIdType.MESH


def layer_norm(values_in):
    average = jnp.mean(values_in, axis=-1, keepdims=True)
    centered = values_in - average
    variance = jnp.mean(centered * centered, axis=-1, keepdims=True)
    return centered * lax.rsqrt(variance + 1e-05)


def mul(left, right):
    return jnp.dot(left, right, preferred_element_type=F32)


def mul_t(left, right):
    return lax.dot_general(left, right, (((1,), (1,)), ((), ())), preferred_element_type=F32)


def kernel(
    rows_n,
    length_hbm,
    pair_hbm,
    w_tri_in_hbm,
    w_tri_out_hbm,
    w_att_hbm,
    w_bias_hbm,
    w_att_out_hbm,
    w_up_hbm,
    w_down_hbm,
    out_ref,
    length_ref,
    pair_ref,
    w_tri_in,
    w_tri_out,
    w_att,
    w_bias,
    w_att_out,
    w_up,
    w_down,
    load_sem,
    normed,
    right_all,
    left_f,
    pair_other,
    gate,
    acc,
    part_out,
    part_in,
    cells_f,
    scores_s,
    slab,
    keys_s,
    values_s,
    queries_s,
    att_gate,
    bias_own,
    bias_all,
    bias_f,
    ring_send,
    ring_recv,
    part_send,
    part_recv,
    pair_send,
    pair_recv,
    bias_send,
    bias_recv,
):
    rows, cols, channels = pair_ref.shape
    full = 2 * cols
    padded = slab.shape[1]
    slab_rows = rows // 2
    hidden_units = w_down.shape[0]
    head_size = channels // HEADS
    peers = 2 * rows_n
    half_ring = rows_n // 2
    pair_cells = 2 * cols
    cells = rows * cols
    pairs = rows // 2
    cuts = [0, (pairs + 2) // 4, (pairs + 1) // 2, (3 * pairs + 3) // 4, pairs]
    parts = tuple((a, b - a) for a, b in zip(cuts[:-1], cuts[1:]))
    orders = ((0, 1, 2, 3), (2, 3, 0, 1))
    early = scores_s.shape[1] == full
    snake = rows_n <= 8

    def loop(count, step):
        lax.fori_loop(0, count, step, 0, unroll=early)


    row = lax.axis_index("row")
    col = lax.axis_index("col")
    me = row * 2 + col

    def place(r):
        if not snake:
            return r
        return jnp.where(r % 2 == 0, r // 2, rows_n - 1 - r // 2)

    def owner_at(p):
        p = lax.rem(p + 2 * rows_n, rows_n)
        if not snake:
            return p
        return jnp.where(p < rows_n // 2, 2 * p, 2 * (rows_n - p) - 1)

    pos = place(row)
    nexts = (owner_at(pos + 1), owner_at(pos - 1))

    barrier = pltpu.get_barrier_semaphore()
    for way in range(2):
        pl.semaphore_signal(
            barrier, inc=1, device_id={"row": nexts[way]}, device_id_type=MESH
        )
    pl.semaphore_signal(barrier, inc=1, device_id={"col": 1 - col}, device_id_type=MESH)

    operands = (
        (length_hbm, length_ref),
        (pair_hbm, pair_ref),
        (w_tri_in_hbm, w_tri_in),
        (w_tri_out_hbm, w_tri_out),
        (w_bias_hbm, w_bias),
        (w_att_hbm, w_att),
        (w_att_out_hbm, w_att_out),
        (w_up_hbm, w_up),
        (w_down_hbm, w_down),
    )
    loads = [
        pltpu.make_async_copy(src, dst, load_sem.at[k]) for k, (src, dst) in enumerate(operands)
    ]
    for load in loads:
        load.start()
    for load in loads[:3]:
        load.wait()
    length = length_ref[0]
    row_off = row * rows
    col_off = col * cols
    flat = lax.broadcasted_iota(jnp.int32, (pair_cells, channels), 0)
    second_row = (flat >= cols).astype(jnp.int32)
    col_ok = col_off + flat - cols * second_row < length

    def keep_of(p):
        return col_ok & (row_off + 2 * p + second_row < length)

    def right_step(p, carry):
        block = pair_ref[pl.ds(2 * p, 2)].astype(F32).reshape(pair_cells, channels)
        norm = layer_norm(block).astype(BF16)
        at = pl.ds(pl.multiple_of(p * pair_cells, 16), pair_cells)
        normed[at, :] = norm
        proj = mul(norm, w_tri_in[:, 2 * channels : 4 * channels])
        edge = jax.nn.sigmoid(proj[:, channels:]) * proj[:, :channels]
        to = pl.ds(pl.multiple_of(row * cells + p * pair_cells, 16), pair_cells)
        right_all[to, :] = jnp.where(keep_of(p), edge, 0.0).astype(BF16)
        return carry

    def ring_copy(way, dist, part, owner):
        start, count = parts[part]
        at = pl.ds(
            pl.multiple_of(owner * cells + start * pair_cells, 16), count * pair_cells
        )
        return pltpu.make_async_remote_copy(
            src_ref=right_all.at[at],
            dst_ref=right_all.at[at],
            send_sem=ring_send.at[way, dist, part],
            recv_sem=ring_recv.at[way, dist, part],
            device_id={"row": nexts[way]},
            device_id_type=MESH,
        )

    pair_copy = pltpu.make_async_remote_copy(
        src_ref=pair_ref.at[pl.ds((1 - col) * slab_rows, slab_rows)],
        dst_ref=pair_other,
        send_sem=pair_send,
        recv_sem=pair_recv,
        device_id={"col": 1 - col},
        device_id_type=MESH,
    )

    lax.fori_loop(0, pairs, right_step, 0)
    pl.semaphore_wait(barrier, 3)
    for turn in range(4):
        for way in range(2):
            ring_copy(way, 1, orders[way][turn], row).start()
    pair_copy.start()

    def left_step(p, carry):
        at = pl.ds(pl.multiple_of(p * pair_cells, 16), pair_cells)
        proj = mul(normed[at, :], w_tri_in[:, : 2 * channels])
        edge = jax.nn.sigmoid(proj[:, channels:]) * proj[:, :channels]
        edge = jnp.where(keep_of(p), edge, 0.0).astype(BF16).astype(F32)
        left_f[pl.ds(2 * p, 2)] = edge.reshape(2, cols, channels)
        return carry

    lax.fori_loop(0, rows // 2, left_step, 0)

    def part_copy(part, owner):
        start, count = parts[part]
        at = pl.ds(pl.multiple_of((owner * rows + 2 * start) * 8, 16), 16 * count)
        return pltpu.make_async_remote_copy(
            src_ref=part_out.at[at],
            dst_ref=part_in.at[at],
            send_sem=part_send.at[owner, part],
            recv_sem=part_recv.at[owner, part],
            device_id={"col": 1 - col},
            device_id_type=MESH,
        )

    def tri_part(part, owner):
        start, count = parts[part]

        def step(p, carry):
            at = pl.ds(pl.multiple_of(owner * cells + p * pair_cells, 16), pair_cells)
            both = right_all[at, :].astype(F32).reshape(2, cols, channels)
            for side, ref in ((1 - col, part_out), (col, acc)):
                block = left_f[pl.ds(side * slab_rows, slab_rows)]
                for t in range(2):
                    total = jnp.sum(block * both[t][None], axis=1)
                    to = pl.multiple_of((owner * rows + 2 * p + t) * 8, 8)
                    ref[pl.ds(to, slab_rows), :] = total
            return carry

        lax.fori_loop(start, start + count, step, 0)
        part_copy(part, owner).start()

    for part in range(4):
        tri_part(part, row)

    pair_copy.wait_recv()

    def whole_row(i):
        own = pair_ref[col * slab_rows + i].astype(F32)
        other = pair_other[i].astype(F32)
        low = jnp.where(col == 0, own, other)
        high = jnp.where(col == 0, other, own)
        return jnp.concatenate([low, high], axis=0)

    def gate_step(i, carry):
        whole = whole_row(i)
        at = pl.ds(i, full, stride=8)
        cells_f[at, :] = whole
        norm = layer_norm(whole).astype(BF16)
        gate[at, :] = jax.nn.sigmoid(mul(norm, w_tri_in[:, 4 * channels :]))
        return carry

    lax.fori_loop(0, slab_rows, gate_step, 0)
    loads[3].wait()

    def finish(owner):
        for part in range(4):
            part_copy(part, owner).wait_recv()
        at = pl.ds(pl.multiple_of(owner * rows * 8, 16), rows * 8)
        tri_norm = layer_norm(acc[at, :] + part_in[at, :]).astype(BF16)
        fresh = cells_f[at, :] + gate[at, :] * mul(tri_norm, w_tri_out[...])
        fresh = fresh.astype(BF16).astype(F32)
        acc[at, :] = fresh
        cells_f[at, :] = layer_norm(fresh)

    def ring_step(s, carry):
        owners = (owner_at(pos - s), owner_at(pos + s))
        for turn in range(4):
            for way in range(2):
                part = orders[way][turn]
                ring_copy(way, s, part, owners[way]).wait_recv()
                if turn < 2:
                    ring_copy(way, s + 1, part, owners[way]).start()
                else:

                    @pl.when(s < half_ring - 1)
                    def _():
                        ring_copy(way, s + 1, part, owners[way]).start()

            for way in range(2):
                tri_part(orders[way][turn], owners[way])
        finish(owner_at(pos - s + 1))

        @pl.when(s > 1)
        def _():
            finish(owner_at(pos + s - 1))

        return carry

    lax.fori_loop(1, half_ring, ring_step, 0)
    finish(owner_at(pos - half_ring + 1))
    finish(owner_at(pos + half_ring - 1))
    far = owner_at(pos + half_ring)
    for turn in range(2):
        for way in range(2):
            ring_copy(way, half_ring, orders[way][turn], far).wait_recv()
            tri_part(orders[way][turn], far)
    finish(far)
    for load in loads[4:]:
        load.wait()

    bias_own[...] = jnp.zeros_like(bias_own)
    bias_w = jnp.concatenate(
        [w_bias[...].astype(F32), jnp.zeros((16 - HEADS, channels), F32)], axis=0
    ).astype(BF16)

    def norm_step(i, carry):
        norm = cells_f[pl.ds(i, full, stride=8), :]
        if padded > full:
            norm = jnp.concatenate([norm, jnp.zeros((padded - full, channels), F32)], axis=0)
        norm = norm.astype(BF16)
        slab[i] = norm
        bias = mul_t(bias_w, norm)
        for h in range(HEADS):
            bias_own[pl.ds(8 * h + i, 1), :] = bias[h : h + 1]
        return carry

    loop(slab_rows, norm_step)
    bias_all[me] = bias_own[...].astype(BF16)

    def bias_copy(t):
        peer = lax.rem(me + t, peers)
        return pltpu.make_async_remote_copy(
            src_ref=bias_all.at[me],
            dst_ref=bias_all.at[me],
            send_sem=bias_send.at[t],
            recv_sem=bias_recv.at[t],
            device_id={"row": peer // 2, "col": peer % 2},
            device_id_type=MESH,
        )

    def bias_arrival(t):
        peer = lax.rem(me + peers - t, peers)
        return pltpu.make_async_remote_copy(
            src_ref=bias_all.at[peer],
            dst_ref=bias_all.at[peer],
            send_sem=bias_send.at[t],
            recv_sem=bias_recv.at[t],
            device_id={"row": peer // 2, "col": peer % 2},
            device_id_type=MESH,
        )

    def bias_start(t, carry):
        bias_copy(t).start()
        return carry

    lax.fori_loop(1, peers, bias_start, 0)

    head_of = lax.broadcasted_iota(jnp.int32, (full, channels), 1) // head_size

    def score(h, query, key):
        query = jnp.where(head_of == h, query.astype(F32), 0.0).astype(BF16)
        return mul_t(query, key)

    def att_step(i, carry):
        proj = mul(slab[i], w_att[...])
        query = (proj[:full, :channels] * head_size ** (-0.5)).astype(BF16)
        key = proj[:, channels : 2 * channels].astype(BF16)
        if early:
            for h in range(HEADS):
                scores_s[i * HEADS + h] = score(h, query, key)
        else:
            queries_s[i] = query
            keys_s[i] = key
        values_s[i, :, :channels] = proj[:, 2 * channels : 3 * channels].astype(BF16)
        values_s[i, :, channels:] = jnp.ones((padded, channels), BF16)
        att_gate[i] = jax.nn.sigmoid(proj[:full, 3 * channels :])
        return carry

    loop(slab_rows, att_step)

    def bias_wait(t, carry):
        bias_arrival(t).wait_recv()
        return carry

    lax.fori_loop(1, peers, bias_wait, 0)
    key_ok = lax.broadcasted_iota(jnp.int32, (slab_rows, padded), 1) < length
    for peer in range(peers):
        block = bias_all[peer].astype(F32)
        for h in range(HEADS):
            bias_f[h, peer * slab_rows : (peer + 1) * slab_rows, :] = jnp.where(
                key_ok, block[8 * h : 8 * h + slab_rows], -1000000000.0
            )

    def row_step(i, carry):
        value = values_s[i]
        top = jnp.zeros((full, channels), F32)
        bottom = jnp.zeros((full, channels), F32)
        for h in range(HEADS):
            mine = head_of == h
            if early:
                scores = scores_s[i * HEADS + h] + bias_f[h]
            else:
                scores = score(h, queries_s[i], keys_s[i]) + bias_f[h]
            peak = jnp.max(scores, axis=-1, keepdims=True)
            expo = jnp.exp(scores - peak).astype(BF16)
            mixed = mul(expo, value)
            top = jnp.where(mine, mixed[:, :channels], top)
            bottom = jnp.where(mine, mixed[:, channels:], bottom)
        gated = (att_gate[i] * (top / bottom)).astype(BF16)
        second = (acc[pl.ds(i, full, stride=8), :] + mul(gated, w_att_out[...])).astype(BF16).astype(F32)
        hidden = mul(layer_norm(second).astype(BF16), w_up[...])
        activated = jax.nn.silu(hidden[:, :hidden_units]) * hidden[:, hidden_units:]
        result = second + mul(activated.astype(BF16), w_down[...])
        out_ref[i] = result
        return carry

    loop(slab_rows, row_step)

    pair_copy.wait_send()

    def ring_drain(s, carry):
        owners = (owner_at(pos - s), owner_at(pos + s))
        for way in range(2):
            for part in range(4):
                ring_copy(way, s + 1, part, owners[way]).wait_send()
        return carry

    lax.fori_loop(0, half_ring - 1, ring_drain, 0)
    lasts = (owner_at(pos - half_ring + 1), owner_at(pos + half_ring - 1))
    for way in range(2):
        for turn in range(2):
            ring_copy(way, half_ring, orders[way][turn], lasts[way]).wait_send()

    def part_drain(owner, carry):
        for part in range(4):
            part_copy(part, owner).wait_send()
        return carry

    lax.fori_loop(0, rows_n, part_drain, 0)

    def bias_drain(t, carry):
        bias_copy(t).wait_send()
        return carry

    lax.fori_loop(1, peers, bias_drain, 0)


def shards(rows_n, pair, length, w_tri_in, w_tri_out, w_att, w_bias, w_att_out, w_up, w_down):
    rows, cols, channels = pair.shape
    full = 2 * cols
    padded = -(-full // 128) * 128
    slab_rows = rows // 2
    peers = 2 * rows_n
    half_ring = rows_n // 2
    kept = (slab_rows * HEADS, full, padded) if full <= 128 else (1, 8, 128)
    vmem = pl.BlockSpec(memory_space=pltpu.VMEM)
    dma = pltpu.SemaphoreType.DMA
    operands = (pair, w_tri_in, w_tri_out, w_att, w_bias.T, w_att_out, w_up, w_down)
    result = pl.pallas_call(
        functools.partial(kernel, rows_n),
        out_shape=jax.ShapeDtypeStruct((slab_rows, full, channels), F32),
        in_specs=[pl.BlockSpec(memory_space=pl.ANY)] * 9,
        out_specs=vmem,
        scratch_shapes=[
            pltpu.SMEM(length.shape, jnp.int32),
            *(pltpu.VMEM(operand.shape, BF16) for operand in operands),
            dma((9,)),
            pltpu.VMEM((rows * cols, channels), BF16),
            pltpu.VMEM((rows_n * rows * cols, channels), BF16),
            pltpu.VMEM((rows, cols, channels), F32),
            pltpu.VMEM((slab_rows, cols, channels), BF16),
            pltpu.VMEM((full * 8, channels), F32),
            pltpu.VMEM((full * 8, channels), F32),
            pltpu.VMEM((full * 8, channels), F32),
            pltpu.VMEM((full * 8, channels), F32),
            pltpu.VMEM((full * 8, channels), F32),
            pltpu.VMEM(kept, F32),
            pltpu.VMEM((slab_rows, padded, channels), BF16),
            pltpu.VMEM((slab_rows, padded, channels), BF16),
            pltpu.VMEM((slab_rows, padded, 2 * channels), BF16),
            pltpu.VMEM((slab_rows, full, channels), BF16),
            pltpu.VMEM((slab_rows, full, channels), F32),
            pltpu.VMEM((HEADS * 8, padded), F32),
            pltpu.VMEM((peers, HEADS * 8, padded), BF16),
            pltpu.VMEM((HEADS, full, padded), F32),
            dma((2, half_ring + 1, 4)),
            dma((2, half_ring + 1, 4)),
            dma((rows_n, 4)),
            dma((rows_n, 4)),
            dma,
            dma,
            dma((peers,)),
            dma((peers,)),
        ],
        compiler_params=pltpu.CompilerParams(
            collective_id=0, has_side_effects=True, vmem_limit_bytes=60 * 2**20
        ),
    )(length, *operands)
    return result.astype(BF16)


def solution(mesh):
    placed = (P(("dom", "row"), "col", None), P("dom"), P(), P(), P(), P(), P(), P(), P())
    return jax.shard_map(
        functools.partial(shards, mesh.shape["row"]),
        mesh=mesh,
        in_specs=placed,
        out_specs=P(("dom", "row", "col"), None, None),
        check_vma=False,
    )
```

```python
import functools

import jax
import jax.numpy as jnp
from jax import lax
from jax.experimental import pallas as pl
from jax.experimental.pallas import tpu as pltpu
from jax.sharding import PartitionSpec as P

HEADS = 4
F32 = jnp.float32
BF16 = jnp.bfloat16
MESH = pl.DeviceIdType.MESH


def layer_norm(values_in):
    average = jnp.mean(values_in, axis=-1, keepdims=True)
    centered = values_in - average
    variance = jnp.mean(centered * centered, axis=-1, keepdims=True)
    return centered * lax.rsqrt(variance + 1e-05)


def mul(left, right):
    return jnp.dot(left, right, preferred_element_type=F32)


def mul_t(left, right):
    return lax.dot_general(left, right, (((1,), (1,)), ((), ())), preferred_element_type=F32)


def kernel(
    rows_n,
    length_hbm,
    pair_hbm,
    w_tri_in_hbm,
    w_tri_out_hbm,
    w_att_hbm,
    w_bias_hbm,
    w_att_out_hbm,
    w_up_hbm,
    w_down_hbm,
    out_ref,
    length_ref,
    pair_ref,
    w_tri_in,
    w_tri_out,
    w_att,
    w_bias,
    w_att_out,
    w_up,
    w_down,
    load_sem,
    normed,
    right_all,
    left_f,
    pair_other,
    gate,
    acc,
    part_out,
    part_in,
    cells_f,
    scores_s,
    slab,
    keys_s,
    values_s,
    queries_s,
    att_gate,
    bias_own,
    bias_all,
    bias_f,
    ring_send,
    ring_recv,
    part_send,
    part_recv,
    pair_send,
    pair_recv,
    bias_send,
    bias_recv,
):
    rows, cols, channels = pair_ref.shape
    full = 2 * cols
    padded = slab.shape[1]
    slab_rows = rows // 2
    hidden_units = w_down.shape[0]
    head_size = channels // HEADS
    peers = 2 * rows_n
    half_ring = rows_n // 2
    pair_cells = 2 * cols
    cells = rows * cols
    pairs = rows // 2
    cuts = [0, (pairs + 2) // 4, (pairs + 1) // 2, (3 * pairs + 3) // 4, pairs]
    parts = tuple((a, b - a) for a, b in zip(cuts[:-1], cuts[1:]))
    orders = ((0, 1, 2, 3), (2, 3, 0, 1))
    early = scores_s.shape[1] == full
    snake = rows_n <= 8

    def loop(count, step):
        lax.fori_loop(0, count, step, 0, unroll=early)


    row = lax.axis_index("row")
    col = lax.axis_index("col")
    me = row * 2 + col

    def place(r):
        if not snake:
            return r
        return jnp.where(r % 2 == 0, r // 2, rows_n - 1 - r // 2)

    def owner_at(p):
        p = lax.rem(p + 2 * rows_n, rows_n)
        if not snake:
            return p
        return jnp.where(p < rows_n // 2, 2 * p, 2 * (rows_n - p) - 1)

    pos = place(row)
    nexts = (owner_at(pos + 1), owner_at(pos - 1))

    barrier = pltpu.get_barrier_semaphore()
    for way in range(2):
        pl.semaphore_signal(
            barrier, inc=1, device_id={"row": nexts[way]}, device_id_type=MESH
        )
    pl.semaphore_signal(barrier, inc=1, device_id={"col": 1 - col}, device_id_type=MESH)

    operands = (
        (length_hbm, length_ref),
        (pair_hbm, pair_ref),
        (w_tri_in_hbm, w_tri_in),
        (w_tri_out_hbm, w_tri_out),
        (w_bias_hbm, w_bias),
        (w_att_hbm, w_att),
        (w_att_out_hbm, w_att_out),
        (w_up_hbm, w_up),
        (w_down_hbm, w_down),
    )
    loads = [
        pltpu.make_async_copy(src, dst, load_sem.at[k]) for k, (src, dst) in enumerate(operands)
    ]
    for load in loads:
        load.start()
    for load in loads[:3]:
        load.wait()
    length = length_ref[0]
    row_off = row * rows
    col_off = col * cols
    flat = lax.broadcasted_iota(jnp.int32, (pair_cells, channels), 0)
    second_row = (flat >= cols).astype(jnp.int32)
    col_ok = col_off + flat - cols * second_row < length

    def keep_of(p):
        return col_ok & (row_off + 2 * p + second_row < length)

    def right_step(p, carry):
        block = pair_ref[pl.ds(2 * p, 2)].astype(F32).reshape(pair_cells, channels)
        norm = layer_norm(block).astype(BF16)
        at = pl.ds(pl.multiple_of(p * pair_cells, 16), pair_cells)
        normed[at, :] = norm
        proj = mul(norm, w_tri_in[:, 2 * channels : 4 * channels])
        edge = jax.nn.sigmoid(proj[:, channels:]) * proj[:, :channels]
        to = pl.ds(pl.multiple_of(row * cells + p * pair_cells, 16), pair_cells)
        right_all[to, :] = jnp.where(keep_of(p), edge, 0.0).astype(BF16)
        return carry

    def ring_copy(way, dist, part, owner):
        start, count = parts[part]
        at = pl.ds(
            pl.multiple_of(owner * cells + start * pair_cells, 16), count * pair_cells
        )
        return pltpu.make_async_remote_copy(
            src_ref=right_all.at[at],
            dst_ref=right_all.at[at],
            send_sem=ring_send.at[way, dist, part],
            recv_sem=ring_recv.at[way, dist, part],
            device_id={"row": nexts[way]},
            device_id_type=MESH,
        )

    pair_copy = pltpu.make_async_remote_copy(
        src_ref=pair_ref.at[pl.ds((1 - col) * slab_rows, slab_rows)],
        dst_ref=pair_other,
        send_sem=pair_send,
        recv_sem=pair_recv,
        device_id={"col": 1 - col},
        device_id_type=MESH,
    )

    lax.fori_loop(0, pairs, right_step, 0)
    pl.semaphore_wait(barrier, 3)
    for turn in range(4):
        for way in range(2):
            ring_copy(way, 1, orders[way][turn], row).start()
    pair_copy.start()

    def left_step(p, carry):
        at = pl.ds(pl.multiple_of(p * pair_cells, 16), pair_cells)
        proj = mul(normed[at, :], w_tri_in[:, : 2 * channels])
        edge = jax.nn.sigmoid(proj[:, channels:]) * proj[:, :channels]
        edge = jnp.where(keep_of(p), edge, 0.0).astype(BF16).astype(F32)
        left_f[pl.ds(2 * p, 2)] = edge.reshape(2, cols, channels)
        return carry

    lax.fori_loop(0, rows // 2, left_step, 0)

    def part_copy(part, owner):
        start, count = parts[part]
        at = pl.ds(pl.multiple_of((owner * rows + 2 * start) * 8, 16), 16 * count)
        return pltpu.make_async_remote_copy(
            src_ref=part_out.at[at],
            dst_ref=part_in.at[at],
            send_sem=part_send.at[owner, part],
            recv_sem=part_recv.at[owner, part],
            device_id={"col": 1 - col},
            device_id_type=MESH,
        )

    def tri_part(part, owner):
        start, count = parts[part]

        def step(p, carry):
            at = pl.ds(pl.multiple_of(owner * cells + p * pair_cells, 16), pair_cells)
            both = right_all[at, :].astype(F32).reshape(2, cols, channels)
            for side, ref in ((1 - col, part_out), (col, acc)):
                block = left_f[pl.ds(side * slab_rows, slab_rows)]
                for t in range(2):
                    total = jnp.sum(block * both[t][None], axis=1)
                    to = pl.multiple_of((owner * rows + 2 * p + t) * 8, 8)
                    ref[pl.ds(to, slab_rows), :] = total
            return carry

        lax.fori_loop(start, start + count, step, 0)
        part_copy(part, owner).start()

    for part in range(4):
        tri_part(part, row)

    pair_copy.wait_recv()

    def whole_row(i):
        own = pair_ref[col * slab_rows + i].astype(F32)
        other = pair_other[i].astype(F32)
        low = jnp.where(col == 0, own, other)
        high = jnp.where(col == 0, other, own)
        return jnp.concatenate([low, high], axis=0)

    def gate_step(i, carry):
        whole = whole_row(i)
        at = pl.ds(i, full, stride=8)
        cells_f[at, :] = whole
        norm = layer_norm(whole).astype(BF16)
        gate[at, :] = jax.nn.sigmoid(mul(norm, w_tri_in[:, 4 * channels :]))
        return carry

    lax.fori_loop(0, slab_rows, gate_step, 0)
    loads[3].wait()

    def finish(owner):
        for part in range(4):
            part_copy(part, owner).wait_recv()
        at = pl.ds(pl.multiple_of(owner * rows * 8, 16), rows * 8)
        tri_norm = layer_norm(acc[at, :] + part_in[at, :]).astype(BF16)
        fresh = cells_f[at, :] + gate[at, :] * mul(tri_norm, w_tri_out[...])
        fresh = fresh.astype(BF16).astype(F32)
        acc[at, :] = fresh
        cells_f[at, :] = layer_norm(fresh)

    def ring_step(s, carry):
        owners = (owner_at(pos - s), owner_at(pos + s))
        for turn in range(4):
            for way in range(2):
                part = orders[way][turn]
                ring_copy(way, s, part, owners[way]).wait_recv()
                if turn < 2:
                    ring_copy(way, s + 1, part, owners[way]).start()
                else:

                    @pl.when(s < half_ring - 1)
                    def _():
                        ring_copy(way, s + 1, part, owners[way]).start()

            for way in range(2):
                tri_part(orders[way][turn], owners[way])
        finish(owner_at(pos - s + 1))

        @pl.when(s > 1)
        def _():
            finish(owner_at(pos + s - 1))

        return carry

    lax.fori_loop(1, half_ring, ring_step, 0)
    finish(owner_at(pos - half_ring + 1))
    finish(owner_at(pos + half_ring - 1))
    far = owner_at(pos + half_ring)
    for turn in range(2):
        for way in range(2):
            ring_copy(way, half_ring, orders[way][turn], far).wait_recv()
            tri_part(orders[way][turn], far)
    finish(far)
    for load in loads[4:]:
        load.wait()

    bias_own[...] = jnp.zeros_like(bias_own)
    bias_w = jnp.concatenate(
        [w_bias[...].astype(F32), jnp.zeros((16 - HEADS, channels), F32)], axis=0
    ).astype(BF16)

    def norm_step(i, carry):
        norm = cells_f[pl.ds(i, full, stride=8), :]
        if padded > full:
            norm = jnp.concatenate([norm, jnp.zeros((padded - full, channels), F32)], axis=0)
        norm = norm.astype(BF16)
        slab[i] = norm
        bias = mul_t(bias_w, norm)
        for h in range(HEADS):
            bias_own[pl.ds(8 * h + i, 1), :] = bias[h : h + 1]
        return carry

    loop(slab_rows, norm_step)
    bias_all[me] = bias_own[...].astype(BF16)

    def bias_move(slot, sem, peer):
        return pltpu.make_async_remote_copy(
            src_ref=bias_all.at[slot],
            dst_ref=bias_all.at[slot],
            send_sem=bias_send.at[sem],
            recv_sem=bias_recv.at[sem],
            device_id=peer,
            device_id_type=MESH,
        )

    def bias_copy(t):
        return bias_move(me, t, {"row": lax.rem(row + t, rows_n)})

    def bias_arrival(t):
        source = lax.rem(row + rows_n - t, rows_n)
        return bias_move(source * 2 + col, t, {"row": source})

    def bias_share(t, core):
        source = lax.rem(row + rows_n - t, rows_n)
        return bias_move(source * 2 + core, rows_n + t, {"col": 1 - col})

    def bias_start(t, carry):
        bias_copy(t).start()
        return carry

    lax.fori_loop(1, rows_n, bias_start, 0)
    bias_share(0, col).start()

    head_of = lax.broadcasted_iota(jnp.int32, (full, channels), 1) // head_size

    def score(h, query, key):
        query = jnp.where(head_of == h, query.astype(F32), 0.0).astype(BF16)
        return mul_t(query, key)

    def att_step(i, carry):
        proj = mul(slab[i], w_att[...])
        query = (proj[:full, :channels] * head_size ** (-0.5)).astype(BF16)
        key = proj[:, channels : 2 * channels].astype(BF16)
        if early:
            for h in range(HEADS):
                scores_s[i * HEADS + h] = score(h, query, key)
        else:
            queries_s[i] = query
            keys_s[i] = key
        values_s[i, :, :channels] = proj[:, 2 * channels : 3 * channels].astype(BF16)
        values_s[i, :, channels:] = jnp.ones((padded, channels), BF16)
        att_gate[i] = jax.nn.sigmoid(proj[:full, 3 * channels :])
        return carry

    loop(slab_rows, att_step)

    def bias_pass(t, carry):
        bias_arrival(t).wait_recv()
        bias_share(t, col).start()
        return carry

    def bias_wait(t, carry):
        bias_share(t, 1 - col).wait_recv()
        return carry

    lax.fori_loop(1, rows_n, bias_pass, 0)
    lax.fori_loop(0, rows_n, bias_wait, 0)
    key_ok = lax.broadcasted_iota(jnp.int32, (slab_rows, padded), 1) < length
    for peer in range(peers):
        block = bias_all[peer].astype(F32)
        for h in range(HEADS):
            bias_f[h, peer * slab_rows : (peer + 1) * slab_rows, :] = jnp.where(
                key_ok, block[8 * h : 8 * h + slab_rows], -1000000000.0
            )

    def row_step(i, carry):
        value = values_s[i]
        top = jnp.zeros((full, channels), F32)
        bottom = jnp.zeros((full, channels), F32)
        for h in range(HEADS):
            mine = head_of == h
            if early:
                scores = scores_s[i * HEADS + h] + bias_f[h]
            else:
                scores = score(h, queries_s[i], keys_s[i]) + bias_f[h]
            peak = jnp.max(scores, axis=-1, keepdims=True)
            expo = jnp.exp(scores - peak).astype(BF16)
            mixed = mul(expo, value)
            top = jnp.where(mine, mixed[:, :channels], top)
            bottom = jnp.where(mine, mixed[:, channels:], bottom)
        gated = (att_gate[i] * (top / bottom)).astype(BF16)
        second = (acc[pl.ds(i, full, stride=8), :] + mul(gated, w_att_out[...])).astype(BF16).astype(F32)
        hidden = mul(layer_norm(second).astype(BF16), w_up[...])
        activated = jax.nn.silu(hidden[:, :hidden_units]) * hidden[:, hidden_units:]
        result = second + mul(activated.astype(BF16), w_down[...])
        out_ref[i] = result
        return carry

    loop(slab_rows, row_step)

    pair_copy.wait_send()

    def ring_drain(s, carry):
        owners = (owner_at(pos - s), owner_at(pos + s))
        for way in range(2):
            for part in range(4):
                ring_copy(way, s + 1, part, owners[way]).wait_send()
        return carry

    lax.fori_loop(0, half_ring - 1, ring_drain, 0)
    lasts = (owner_at(pos - half_ring + 1), owner_at(pos + half_ring - 1))
    for way in range(2):
        for turn in range(2):
            ring_copy(way, half_ring, orders[way][turn], lasts[way]).wait_send()

    def part_drain(owner, carry):
        for part in range(4):
            part_copy(part, owner).wait_send()
        return carry

    lax.fori_loop(0, rows_n, part_drain, 0)

    def bias_drain(t, carry):
        bias_copy(t).wait_send()
        bias_share(t, col).wait_send()
        return carry

    bias_share(0, col).wait_send()
    lax.fori_loop(1, rows_n, bias_drain, 0)


def shards(rows_n, pair, length, w_tri_in, w_tri_out, w_att, w_bias, w_att_out, w_up, w_down):
    rows, cols, channels = pair.shape
    full = 2 * cols
    padded = -(-full // 128) * 128
    slab_rows = rows // 2
    peers = 2 * rows_n
    half_ring = rows_n // 2
    kept = (slab_rows * HEADS, full, padded) if full <= 128 else (1, 8, 128)
    vmem = pl.BlockSpec(memory_space=pltpu.VMEM)
    dma = pltpu.SemaphoreType.DMA
    operands = (pair, w_tri_in, w_tri_out, w_att, w_bias.T, w_att_out, w_up, w_down)
    result = pl.pallas_call(
        functools.partial(kernel, rows_n),
        out_shape=jax.ShapeDtypeStruct((slab_rows, full, channels), F32),
        in_specs=[pl.BlockSpec(memory_space=pl.ANY)] * 9,
        out_specs=vmem,
        scratch_shapes=[
            pltpu.SMEM(length.shape, jnp.int32),
            *(pltpu.VMEM(operand.shape, BF16) for operand in operands),
            dma((9,)),
            pltpu.VMEM((rows * cols, channels), BF16),
            pltpu.VMEM((rows_n * rows * cols, channels), BF16),
            pltpu.VMEM((rows, cols, channels), F32),
            pltpu.VMEM((slab_rows, cols, channels), BF16),
            pltpu.VMEM((full * 8, channels), F32),
            pltpu.VMEM((full * 8, channels), F32),
            pltpu.VMEM((full * 8, channels), F32),
            pltpu.VMEM((full * 8, channels), F32),
            pltpu.VMEM((full * 8, channels), F32),
            pltpu.VMEM(kept, F32),
            pltpu.VMEM((slab_rows, padded, channels), BF16),
            pltpu.VMEM((slab_rows, padded, channels), BF16),
            pltpu.VMEM((slab_rows, padded, 2 * channels), BF16),
            pltpu.VMEM((slab_rows, full, channels), BF16),
            pltpu.VMEM((slab_rows, full, channels), F32),
            pltpu.VMEM((HEADS * 8, padded), F32),
            pltpu.VMEM((peers, HEADS * 8, padded), BF16),
            pltpu.VMEM((HEADS, full, padded), F32),
            dma((2, half_ring + 1, 4)),
            dma((2, half_ring + 1, 4)),
            dma((rows_n, 4)),
            dma((rows_n, 4)),
            dma,
            dma,
            dma((peers,)),
            dma((peers,)),
        ],
        compiler_params=pltpu.CompilerParams(
            collective_id=0, has_side_effects=True, vmem_limit_bytes=60 * 2**20
        ),
    )(length, *operands)
    return result.astype(BF16)


def solution(mesh):
    placed = (P(("dom", "row"), "col", None), P("dom"), P(), P(), P(), P(), P(), P(), P())
    return jax.shard_map(
        functools.partial(shards, mesh.shape["row"]),
        mesh=mesh,
        in_specs=placed,
        out_specs=P(("dom", "row", "col"), None, None),
        check_vma=False,
    )
```
